256 devices in a mesh: tm: 16 (over z, core), head: 16 (over y, x).
Axes of the slice: x: 4, y: 4, z: 8, core: 2. Of those that a mesh axis runs over, the one named last changes fastest.
Arguments:
- start: float32 [2048, 64], P('head'), may hold values from -6 to 6
- latents: float32 [16, 2048, 64], P('tm', 'head'), may hold values from -12 to 12
- time_mod: float32 [16, 3, 3072], P('tm'), may hold values from -3 to 3
- steps_window: int32 [16], P('tm'), may hold values from 0 to 999
- ddim_table: float32 [1000, 2], replicated, may hold values from -0.5 to 0.5
- w_in: bfloat16 [64, 3072], replicated, may hold values from -0.75 to 0.75
- w_qkv: bfloat16 [3, 3072, 3072], P(None, 'head'), may hold values from -0.28867513 to 0.28867513
- w_attn_out: bfloat16 [3072, 3072], P('head'), may hold values from -0.109375 to 0.109375
- w_proj: bfloat16 [3072, 64], replicated, may hold values from -0.109375 to 0.109375
Outputs:
- refreshed: float32 [16, 2048, 64], P('tm', 'head')
- worst_error: float32 [], replicated
The draws below stay inside these ranges and needn't reach their ends.
All inputs are finite; a program needn't handle non-finite values.
Results may differ from the reference program's by a relative error of at most 0.0031.
Values may be sent and summed in bfloat16 or wider, within the bound.
No kernel may reach another device: no remote copies, remote signals or barrier semaphores. Data moves between devices by JAX's collectives and lax.ppermute only.
A program may use at most 128 MiB of HBM per device.

```python
import jax
import jax.numpy as jnp
from jax import lax

D = 3072
HEADS = 48
HD = 64
P_SIZE = 64
STEPS = 1000
SEQ = 2048
WINDOW = 16


def draw_latents(key, part):
    key = jax.random.fold_in(key, 11)
    row_index = jnp.arange(SEQ, dtype=jnp.float32)
    row_ramp = (1.0 + 2.0 * row_index / SEQ)[None, :, None]
    base_draw = jax.random.truncated_normal(key, -4.0, 4.0, (WINDOW, SEQ, P_SIZE), jnp.float32)
    values_out = base_draw * row_ramp
    return jnp.clip(values_out, -12.0, 12.0)


def draw_w_qkv(key, part):
    key = jax.random.fold_in(key, 23)
    first_key, second_key, third_key = jax.random.split(key, 3)
    shape_one = (HEADS * HD, D)
    query_part = jax.random.truncated_normal(first_key, -4.0, 4.0, shape_one, jnp.float32)
    other_part = jax.random.truncated_normal(second_key, -4.0, 4.0, shape_one, jnp.float32)
    value_part = jax.random.truncated_normal(third_key, -4.0, 4.0, shape_one, jnp.float32)
    scale_now = 1.0 / D ** 0.5
    key_part = other_part
    stacked = jnp.stack([query_part, key_part, value_part], 0) * scale_now
    return stacked.astype(jnp.bfloat16)


def plant(entries, stream_key, least, top_value):
    longest = entries.shape.index(max(entries.shape))
    spots = []
    for shift in (0, 1):
        where = [jax.random.randint(jax.random.fold_in(stream_key, axis), (), 0, length) for axis, length in enumerate(entries.shape)]
        where[longest] = (where[longest] + shift) % entries.shape[longest]
        spots.append(tuple(where))
    return entries.at[spots[0]].set(least).at[spots[1]].set(top_value)


def levels(own_key, extent, shards, smallest, high):
    level = 1.0
    for position, blocks in shards:
        heights = jax.random.uniform(jax.random.fold_in(jax.random.fold_in(own_key, 6), position), (blocks,), jnp.float32, smallest / len(shards), high / len(shards))
        level = level * jnp.repeat(jnp.exp(heights), extent[position] // blocks).reshape((-1,) + (1,) * (len(extent) - 1 - position))
    return level


def normal_values(stream_key, dims, width, limit, cuts=(), kind=jnp.bfloat16):
    drawn = width * jax.random.normal(stream_key, dims, jnp.float32)
    if cuts:
        drawn = drawn * levels(stream_key, dims, cuts, -0.22, 0.18)
    return jnp.clip(drawn, -limit, limit).astype(kind)


def setup_inputs(seed: int = 0) -> dict:
    key_list = jax.random.split(jax.random.key(seed), 10)
    return {
        "start": normal_values(key_list[0], (SEQ, P_SIZE), 1.0, 6.0, ((0, 16),), jnp.float32),
        "latents": draw_latents(jax.random.fold_in(key_list[9], 71), 0),
        "time_mod": normal_values(key_list[2], (WINDOW, 3, D), 0.5, 3.0, ((0, 16),), jnp.float32),
        "steps_window": plant(jax.random.randint(key_list[3], (WINDOW,), 0, STEPS), jax.random.fold_in(key_list[3], 1), 0, STEPS - 1).astype(jnp.int32),
        "ddim_table": jnp.clip(jax.random.uniform(key_list[4], (STEPS, 2), jnp.float32, -0.5, 0.5), -0.5, 0.5),
        "w_in": normal_values(key_list[5], (P_SIZE, D), P_SIZE ** -0.5, 0.75),
        "w_qkv": draw_w_qkv(jax.random.fold_in(key_list[9], 71), 0),
        "w_attn_out": normal_values(key_list[7], (HEADS * HD, D), (HEADS * HD) ** -0.5, 0.109375, ((0, 16),)),
        "w_proj": normal_values(key_list[8], (D, P_SIZE), D ** -0.5, 0.109375),
    }


def layer_norm(values_in):
    average = lax.optimization_barrier(jnp.mean(values_in, -1, keepdims=True))
    centred = values_in - average
    variance = lax.optimization_barrier(jnp.mean(centred * centred, -1, keepdims=True))
    return centred * lax.rsqrt(variance + 1e-05)

def block_drift(current, modulation, coefs_row, w_in, w_qkv, w_attn_out, w_proj):
    hidden = jnp.dot(current.astype(jnp.bfloat16), w_in, preferred_element_type=jnp.float32)
    normed = (layer_norm(hidden) * (1.0 + modulation[1]) + modulation[0]).astype(jnp.bfloat16)
    queries = jnp.dot(normed, w_qkv[0].T, preferred_element_type=jnp.float32).astype(jnp.bfloat16)
    keys_all = jnp.dot(normed, w_qkv[1].T, preferred_element_type=jnp.float32).astype(jnp.bfloat16)
    values_all = jnp.dot(normed, w_qkv[2].T, preferred_element_type=jnp.float32).astype(jnp.bfloat16)

    def one_head(head_id):
        offset = (head_id * HD).astype(jnp.int32)
        q_cols = lax.dynamic_slice_in_dim(queries, offset, HD, 1).astype(jnp.float32)
        k_cols = lax.dynamic_slice_in_dim(keys_all, offset, HD, 1).astype(jnp.float32)
        v_cols = lax.dynamic_slice_in_dim(values_all, offset, HD, 1)
        scores = jnp.dot(q_cols, k_cols.T, preferred_element_type=jnp.float32) * HD ** (-0.5)
        weights = jax.nn.softmax(scores, -1).astype(jnp.bfloat16)
        return jnp.dot(weights, v_cols, preferred_element_type=jnp.float32).astype(jnp.bfloat16)
    heads_out = lax.map(one_head, jnp.arange(HEADS, dtype=jnp.int32))
    attended = jnp.transpose(heads_out, (1, 0, 2)).reshape(SEQ, HEADS * HD)
    projected = jnp.dot(attended, w_attn_out, preferred_element_type=jnp.float32)
    residual_sum = hidden + modulation[2] * projected
    predicted = jnp.dot(residual_sum.astype(jnp.bfloat16), w_proj, preferred_element_type=jnp.float32)
    return coefs_row[0] * current + coefs_row[1] * predicted

def reference(start, latents, time_mod, steps_window, ddim_table, w_in, w_qkv, w_attn_out, w_proj):
    currents = jnp.concatenate([start[None], latents[:-1]], 0)
    coefs = ddim_table[steps_window]

    def one_step(packed):
        return block_drift(packed[0], packed[1], packed[2], w_in, w_qkv, w_attn_out, w_proj)
    drifts = lax.map(one_step, (currents, time_mod, coefs))
    refreshed = start[None] + jnp.cumsum(drifts, 0)
    difference = refreshed - latents
    errors = lax.optimization_barrier(jnp.mean(difference * difference, axis=(1, 2)))
    return (refreshed, jnp.max(errors))
```

```python
import functools

import jax
import jax.numpy as jnp
from jax import lax
from jax.experimental import pallas as pl
from jax.experimental.pallas import tpu as pltpu
from jax.sharding import PartitionSpec as P

HD = 64
LANES = 128
LOG2E = 1.4426950408889634
SAFE = 100.0
F32 = jnp.float32
BF16 = jnp.bfloat16
NT = (((1,), (1,)), ((), ()))
MIB = 1 << 20


def lane_ids(shape):
    return lax.broadcasted_iota(jnp.int32, shape, len(shape) - 1)


def row_ids(shape):
    return lax.broadcasted_iota(jnp.int32, shape, 0)


def exact_dot(a, b):
    return jnp.dot(a, b, precision=lax.Precision.HIGHEST, preferred_element_type=F32)


def split_rows(values, before, after):
    head = values.astype(BF16)
    rest = (values - head.astype(F32)).astype(BF16)
    width = values.shape[1]
    parts = []
    for part in (head, rest):
        if before:
            parts.append(jnp.zeros((before, width), BF16))
        parts.append(part)
        if after:
            parts.append(jnp.zeros((after, width), BF16))
    return jnp.concatenate(parts, 0)


def weights_kernel(
    steps_ref, mod_ref, w_in_ref, w_qkv_ref, w_out_ref, w_proj_ref, lat_ref, table_ref,
    params_ref, w_io_ref, lat_pay_ref, coefs_ref, proj_sum, out_sum, io_sum, average,
):
    k = pl.program_id(0)
    local_heads = w_qkv_ref.shape[1] // HD
    cols = w_qkv_ref.shape[2]

    @pl.when(k == 0)
    def _():
        proj_sum[...] = jnp.zeros_like(proj_sum)
        out_sum[...] = jnp.zeros_like(out_sum)
        io_sum[...] = jnp.zeros_like(io_sum)
        average[...] = jnp.mean(w_in_ref[...].astype(F32), -1, keepdims=True)
        table = table_ref[...]
        picked = jnp.where(lane_ids(table.shape) == steps_ref[0], table, 0.0)
        coefs = jnp.broadcast_to(jnp.sum(picked, -1, keepdims=True), (2, LANES))
        c0 = jnp.broadcast_to(coefs[0:1], (8, LANES))
        c1 = jnp.broadcast_to(coefs[1:2], (8, LANES))
        coefs_ref[...] = jnp.concatenate([c0, c1], 0)
        pay = jnp.concatenate([lat_ref[...], c0], 0)
        for i in range(lat_pay_ref.shape[0]):
            lat_pay_ref[i] = pay

    at = pl.ds(pl.multiple_of(k * cols, cols), cols)
    w_in = w_in_ref[:, at]
    shift, scale, gate = mod_ref[0], mod_ref[1], mod_ref[2]
    inner = (w_in.astype(F32) - average[...]) * (1.0 + scale)
    shift_rows = jnp.where(row_ids((8, cols)) == 0, jnp.broadcast_to(shift, (8, cols)), 0.0)
    tokens_in = split_rows(jnp.concatenate([inner, shift_rows], 0), 0, LANES - HD - 8)
    w_qkv = w_qkv_ref[...].reshape(3 * local_heads * HD, cols)
    proj_sum[...] += lax.dot_general(w_qkv, tokens_in, NT, preferred_element_type=F32)
    w_proj = w_proj_ref[...]
    gated = split_rows(w_proj.astype(F32) * gate, HD, 0)
    out_sum[...] += lax.dot_general(w_out_ref[...], gated, NT, preferred_element_type=F32)
    io_sum[...] += lax.dot_general(w_in, w_proj, NT, preferred_element_type=F32)

    @pl.when(k == pl.num_programs(0) - 1)
    def _():
        w_io_ref[...] = io_sum[...]
        proj = proj_sum[:, :LANES] + proj_sum[:, LANES:]
        out = out_sum[:, :LANES] + out_sum[:, LANES:]
        lanes = lane_ids((HD, LANES))
        rows = row_ids((16, LANES))
        extra = jnp.zeros((16, LANES), F32)
        for h in range(local_heads):
            at_q = h * HD
            at_k = (local_heads + h) * HD
            at_v = (2 * local_heads + h) * HD
            q_t = jnp.transpose(proj[at_q : at_q + HD])
            v_t = jnp.transpose(proj[at_v : at_v + HD])
            score = exact_dot(q_t, proj[at_k : at_k + HD]) * (LOG2E * HD**-0.5)
            value = exact_dot(v_t, out[at_q : at_q + HD])
            params_ref[h * HD : (h + 1) * HD] = jnp.where(
                lanes < HD, score[:HD], value[:HD]
            ).astype(BF16)
            score_row = jnp.broadcast_to(score[HD : HD + 1], (16, LANES))
            const_row = jnp.broadcast_to(jnp.transpose(score)[HD : HD + 1], (16, LANES))
            value_row = jnp.broadcast_to(value[HD : HD + 1], (16, LANES))
            extra += jnp.where(rows == h, score_row, 0.0)
            extra += jnp.where(rows == 4 + h, const_row, 0.0)
            extra += jnp.where(rows == 8, value_row, 0.0)
        params_ref[local_heads * HD :] = extra.astype(BF16)


def tokens_kernel(pos_ref, behind_ref, start_ref, w_in_ref, params_ref, pay_ref, own_ref, cur_ref):
    current_t = jnp.where(pos_ref[0] == 0, start_ref[...], behind_ref[...])
    cur_ref[...] = current_t
    rounded = jnp.transpose(current_t).astype(BF16)
    hidden = jnp.dot(rounded, w_in_ref[...], preferred_element_type=F32)
    centred = hidden - jnp.mean(hidden, -1, keepdims=True)
    variance = jnp.mean(centred * centred, -1, keepdims=True)
    scaled = rounded.astype(F32) * lax.rsqrt(variance + 1e-05)
    half = scaled.shape[0] // 2
    own = jnp.concatenate([scaled[:half], scaled[half:]], 1).astype(BF16)
    own_ref[...] = own
    pay = jnp.concatenate([own, params_ref[...]], 0)
    for i in range(pay_ref.shape[0]):
        pay_ref[i] = pay


def unpacked(pairs):
    lanes = lane_ids(pairs.shape)
    one = jnp.where(lanes == HD, 1.0, 0.0)
    first = jnp.where(lanes < HD, pairs, one)
    second = jnp.where(lanes < HD, pltpu.roll(pairs, HD, 1), one)
    return first, second


def attend_kernel(
    all_ref, own_ref, cur_ref, w_io_ref, coefs_ref, pay_ref, keys, keys_t, queries, sums, *, chunk
):
    groups, held, _ = all_ref.shape
    half = own_ref.shape[0]
    tokens = 2 * half
    local_heads = (held - half - 16) // HD
    rows = local_heads * tokens
    pairs = groups * half

    first, second = unpacked(all_ref[:, :half, :].reshape(pairs, LANES).astype(F32))
    keys[:pairs] = first.astype(BF16)
    keys[pairs:] = second.astype(BF16)
    keys_t[:, :pairs] = jnp.transpose(first).astype(BF16)
    keys_t[:, pairs:] = jnp.transpose(second).astype(BF16)
    key_norm = jnp.maximum(
        jnp.max(jnp.sum(first * first, -1, keepdims=True)),
        jnp.max(jnp.sum(second * second, -1, keepdims=True)),
    )
    own = jnp.concatenate(unpacked(own_ref[...].astype(F32)), 0)
    own_x = own[:, :HD].astype(BF16)
    lanes = lane_ids((tokens, LANES))

    def make_queries(j, norm):
        extra = all_ref[j, half + local_heads * HD :].astype(F32)
        for h in range(local_heads):
            at = half + h * HD
            q = jnp.dot(own_x, all_ref[j, at : at + HD], preferred_element_type=F32)
            q += extra[h : h + 1]
            const = jnp.sum(own * extra[4 + h : 5 + h], -1, keepdims=True)
            q = jnp.where(lanes < HD, q, jnp.where(lanes == HD, const, 0.0)).astype(BF16)
            queries[j, h * tokens : (h + 1) * tokens] = q
            q = q.astype(F32)
            norm = jnp.maximum(norm, jnp.sum(q * q, -1, keepdims=True))
        return norm

    query_norm = jnp.max(lax.fori_loop(0, groups, make_queries, jnp.zeros((tokens, 1), F32)))
    safe = query_norm * key_norm <= SAFE * SAFE
    sums[...] = jnp.zeros_like(sums)

    def finish(j, weighted):
        mean = (weighted[:, :HD] / weighted[:, HD : HD + 1]).astype(BF16)
        total = sums[...]
        for h in range(local_heads):
            at = half + h * HD
            total += jnp.dot(
                mean[h * tokens : (h + 1) * tokens],
                all_ref[j, at : at + HD],
                preferred_element_type=F32,
            )
        total += all_ref[j, half + local_heads * HD + 8 : half + local_heads * HD + 16][
            0:1
        ].astype(F32)
        sums[...] = total

    @pl.when(safe)
    def _():
        def step(j, carry):
            q = queries[j]
            weighted = jnp.zeros((rows, LANES), F32)
            for c in range(0, 2 * pairs, chunk):
                s = jnp.dot(q, keys_t[:, c : c + chunk], preferred_element_type=F32)
                p = jnp.exp2(s).astype(BF16)
                weighted += jnp.dot(p, keys[c : c + chunk], preferred_element_type=F32)
            finish(j, weighted)
            return carry

        lax.fori_loop(0, groups, step, 0)

    @pl.when(jnp.logical_not(safe))
    def _():
        def step(j, carry):
            s = jnp.dot(queries[j], keys_t[...], preferred_element_type=F32)
            s = s - jnp.max(s, -1, keepdims=True)
            p = jnp.exp2(s).astype(BF16)
            finish(j, jnp.dot(p, keys[...], preferred_element_type=F32))
            return carry

        lax.fori_loop(0, groups, step, 0)

    attended_t = jnp.transpose(sums[...])[HD:]
    w_io_t = jnp.transpose(w_io_ref[...])
    embedded_t = exact_dot(w_io_t, cur_ref[...].astype(BF16).astype(F32))
    predicted = (coefs_ref[8:9] * (embedded_t + attended_t)).astype(BF16)
    for i in range(pay_ref.shape[0]):
        pay_ref[i] = predicted


def prefix_kernel(pos_ref, pred_ref, lat_ref, start_ref, out_ref, err_ref):
    window = pred_ref.shape[0]
    start = start_ref[...]
    refreshed = start
    own = start
    errors = jnp.zeros((1, LANES), F32)
    lanes = lane_ids((1, LANES))
    for s in range(window):
        current = start if s == 0 else lat_ref[s - 1, :HD]
        refreshed += lat_ref[s, HD : HD + 1] * current + pred_ref[s].astype(F32)
        difference = refreshed - lat_ref[s, :HD]
        error = jnp.sum(difference * difference, axis=(0, 1), keepdims=True)
        errors += jnp.where(lanes == s, error, 0.0)
        own = jnp.where(pos_ref[0] == s, refreshed, own)
    out_ref[...] = own
    for i in range(err_ref.shape[0]):
        err_ref[i] = errors


def vmem():
    return pl.BlockSpec(memory_space=pltpu.VMEM)


def smem():
    return pl.BlockSpec(memory_space=pltpu.SMEM)


def params_of(limit):
    return pltpu.CompilerParams(vmem_limit_bytes=limit * MIB)


def on_device(start, latents, time_mod, steps_window, ddim_table, w_in, w_qkv, w_attn_out, w_proj):
    own_rows = start.shape[0]
    window = lax.axis_size("tm")
    groups = lax.axis_size("head")
    d = w_in.shape[1]
    units = w_qkv.shape[1]
    local_heads = units // HD
    half = own_rows // 2
    held = units + 16
    pos = lax.axis_index("tm").astype(jnp.int32).reshape(1)
    start_t = start.T
    lat_t = latents[0].T
    behind_t = lax.ppermute(lat_t, "tm", [(i, i + 1) for i in range(window - 1)])

    cols = 1024
    whole = lambda *shape: pl.BlockSpec(shape, lambda k: (0,) * len(shape))
    params, w_io, lat_pay, coefs = pl.pallas_call(
        weights_kernel,
        grid=(d // cols,),
        in_specs=[
            smem(),
            pl.BlockSpec((3, 1, cols), lambda k: (0, 0, k)),
            whole(HD, d),
            pl.BlockSpec((3, units, cols), lambda k: (0, 0, k)),
            pl.BlockSpec((units, cols), lambda k: (0, k)),
            pl.BlockSpec((HD, cols), lambda k: (0, k)),
            whole(HD, own_rows),
            whole(2, ddim_table.shape[0]),
        ],
        out_specs=[
            whole(held, LANES),
            whole(HD, HD),
            whole(window, HD + 8, LANES),
            whole(16, LANES),
        ],
        out_shape=[
            jax.ShapeDtypeStruct((held, LANES), BF16),
            jax.ShapeDtypeStruct((HD, HD), F32),
            jax.ShapeDtypeStruct((window, HD + 8, LANES), F32),
            jax.ShapeDtypeStruct((16, LANES), F32),
        ],
        scratch_shapes=[
            pltpu.VMEM((3 * units, 2 * LANES), F32),
            pltpu.VMEM((units, 2 * LANES), F32),
            pltpu.VMEM((HD, HD), F32),
            pltpu.VMEM((HD, 1), F32),
        ],
        compiler_params=params_of(40),
        cost_estimate=pl.CostEstimate(
            flops=2 * d * 4 * units * 256, bytes_accessed=8 * units * d, transcendentals=0
        ),
        name="weights",
    )(
        steps_window,
        time_mod.transpose(1, 0, 2),
        w_in,
        w_qkv,
        w_attn_out,
        w_proj.T,
        lat_t,
        ddim_table.T,
    )

    pay, own, cur_t = pl.pallas_call(
        tokens_kernel,
        in_specs=[smem(), vmem(), vmem(), vmem(), vmem()],
        out_specs=[vmem(), vmem(), vmem()],
        out_shape=[
            jax.ShapeDtypeStruct((groups, half + held, LANES), BF16),
            jax.ShapeDtypeStruct((half, LANES), BF16),
            jax.ShapeDtypeStruct((HD, own_rows), F32),
        ],
        compiler_params=params_of(32),
        name="tokens",
    )(pos, behind_t, start_t, w_in, params)

    gathered = lax.all_to_all(pay, "head", 0, 0, tiled=True)
    lat_all = lax.all_to_all(lat_pay, "tm", 0, 0, tiled=True)

    seq = groups * own_rows
    pred_pay = pl.pallas_call(
        functools.partial(attend_kernel, chunk=256),
        in_specs=[vmem()] * 5,
        out_specs=vmem(),
        out_shape=jax.ShapeDtypeStruct((window, HD, own_rows), BF16),
        scratch_shapes=[
            pltpu.VMEM((seq, LANES), BF16),
            pltpu.VMEM((LANES, seq), BF16),
            pltpu.VMEM((groups, local_heads * own_rows, LANES), BF16),
            pltpu.VMEM((own_rows, LANES), F32),
        ],
        compiler_params=params_of(48),
        cost_estimate=pl.CostEstimate(
            flops=2 * groups * local_heads * own_rows * seq * 512,
            bytes_accessed=4 * MIB,
            transcendentals=groups * local_heads * own_rows * seq,
        ),
        name="attend",
    )(gathered, own, cur_t, w_io, coefs)

    pred_all = lax.all_to_all(pred_pay, "tm", 0, 0, tiled=True)
    refreshed_t, err_pay = pl.pallas_call(
        prefix_kernel,
        in_specs=[smem(), vmem(), vmem(), vmem()],
        out_specs=[vmem(), vmem()],
        out_shape=[
            jax.ShapeDtypeStruct((HD, own_rows), F32),
            jax.ShapeDtypeStruct((groups, 1, LANES), F32),
        ],
        compiler_params=params_of(32),
        name="prefix",
    )(pos, pred_all, lat_all, start_t)
    errors = lax.all_to_all(err_pay, "head", 0, 0, tiled=True)
    worst = jnp.max(jnp.sum(errors, axis=(0, 1)))
    return refreshed_t.T[None], worst / (seq * HD)


def solution(mesh):
    in_specs = (
        P("head", None),
        P("tm", "head", None),
        P("tm", None, None),
        P("tm"),
        P(),
        P(),
        P(None, "head", None),
        P("head", None),
        P(),
    )
    out_specs = (P("tm", "head", None), P())
    return jax.shard_map(
        on_device, mesh=mesh, in_specs=in_specs, out_specs=out_specs, check_vma=False
    )
```

```python
import functools

import jax
import jax.numpy as jnp
from jax import lax
from jax.experimental import pallas as pl
from jax.experimental.pallas import tpu as pltpu
from jax.sharding import PartitionSpec as P

HD = 64
LANES = 128
LOG2E = 1.4426950408889634
SAFE = 100.0
F32 = jnp.float32
BF16 = jnp.bfloat16
NT = (((1,), (1,)), ((), ()))
MIB = 1 << 20


def lane_ids(shape):
    return lax.broadcasted_iota(jnp.int32, shape, len(shape) - 1)


def row_ids(shape):
    return lax.broadcasted_iota(jnp.int32, shape, 0)


def exact_dot(a, b):
    return jnp.dot(a, b, precision=lax.Precision.HIGHEST, preferred_element_type=F32)


def split_rows(values, before, after):
    head = values.astype(BF16)
    rest = (values - head.astype(F32)).astype(BF16)
    width = values.shape[1]
    parts = []
    for part in (head, rest):
        if before:
            parts.append(jnp.zeros((before, width), BF16))
        parts.append(part)
        if after:
            parts.append(jnp.zeros((after, width), BF16))
    return jnp.concatenate(parts, 0)


def weights_kernel(
    mod_ref, w_in_hbm, w_qkv_hbm, w_out_hbm, w_proj_hbm,
    params_ref, w_io_ref, w_in_ref, w_qkv_ref, w_out_ref, w_proj_ref, tokens_in, sems,
):
    local_heads = w_out_ref.shape[0] // HD
    cols = w_in_ref.shape[1]
    moves = [
        (w_in_hbm, w_in_ref),
        (w_qkv_hbm.at[0], w_qkv_ref.at[0]),
        (w_qkv_hbm.at[1], w_qkv_ref.at[1]),
        (w_proj_hbm, w_proj_ref),
        (w_out_hbm, w_out_ref),
        (w_qkv_hbm.at[2], w_qkv_ref.at[2]),
    ]
    copies = [pltpu.make_async_copy(a, b, sems.at[i]) for i, (a, b) in enumerate(moves)]
    for copy in copies:
        copy.start()

    shift, scale, gate = mod_ref[0], mod_ref[1], mod_ref[2]
    copies[0].wait()
    w_in = w_in_ref[...]
    wide = w_in.astype(F32)
    inner = (wide - jnp.mean(wide, -1, keepdims=True)) * (1.0 + scale)
    shift_rows = jnp.where(row_ids((8, cols)) == 0, jnp.broadcast_to(shift, (8, cols)), 0.0)
    tokens_in[...] = split_rows(
        jnp.concatenate([inner, shift_rows], 0), 0, LANES - HD - 8
    )

    def folded(w, by):
        both = lax.dot_general(w, by, NT, preferred_element_type=F32)
        return both[:, :LANES] + both[:, LANES:]

    copies[1].wait()
    proj_q = folded(w_qkv_ref[0], tokens_in[...])
    copies[2].wait()
    proj_k = folded(w_qkv_ref[1], tokens_in[...])
    copies[3].wait()
    w_proj = w_proj_ref[...]
    w_io_ref[...] = lax.dot_general(w_proj, w_in, NT, preferred_element_type=F32)
    gated = split_rows(w_proj.astype(F32) * gate, 0, HD)
    copies[4].wait()
    out = folded(w_out_ref[...], gated)
    copies[5].wait()
    proj_v = folded(w_qkv_ref[2], tokens_in[...])
    lanes = lane_ids((HD, LANES))
    rows = row_ids((16, LANES))
    extra = jnp.zeros((16, LANES), F32)
    maps = []
    for h in range(local_heads):
        at = h * HD
        k_t = jnp.transpose(proj_k[at : at + HD])
        o_t = jnp.transpose(out[at : at + HD])
        score = exact_dot(k_t, proj_q[at : at + HD]) * (LOG2E * HD**-0.5)
        value = exact_dot(o_t, proj_v[at : at + HD])
        maps.append(
            jnp.where(lanes < HD, score[:HD], pltpu.roll(value[:HD], HD, 1)).astype(BF16)
        )
        score_row = jnp.broadcast_to(jnp.transpose(score)[HD : HD + 1], (16, LANES))
        const_row = jnp.broadcast_to(score[HD : HD + 1], (16, LANES))
        value_row = jnp.broadcast_to(jnp.transpose(value)[HD : HD + 1], (16, LANES))
        extra += jnp.where(rows == h, score_row, 0.0)
        extra += jnp.where(rows == 4 + h, const_row, 0.0)
        extra += jnp.where(rows == 8, value_row, 0.0)
    params_ref[...] = jnp.concatenate(maps + [extra.astype(BF16)], 0)


def tokens_kernel(
    pos_ref, behind_ref, start_ref, w_in_ref, params_ref, pay_ref, own_ref, cur_ref, sems
):
    parts = pay_ref.shape[0]
    held = params_ref.shape[0]
    copies = []
    for i in range(parts):
        to = pay_ref.at[i, pl.ds(HD, held)]
        copies.append(pltpu.make_async_copy(params_ref, to, sems.at[0, i]))
        copies[-1].start()
    current_t = jnp.where(pos_ref[0] == 0, start_ref[...], behind_ref[...])
    cur_ref[...] = current_t
    rounded = jnp.transpose(current_t).astype(BF16)
    hidden = jnp.dot(rounded, w_in_ref[...], preferred_element_type=F32)
    centred = hidden - jnp.mean(hidden, -1, keepdims=True)
    variance = jnp.mean(centred * centred, -1, keepdims=True)
    scaled = rounded.astype(F32) * lax.rsqrt(variance + 1e-05)
    own_ref[...] = jnp.transpose(scaled).astype(BF16)
    for i in range(parts):
        to = pay_ref.at[i, pl.ds(0, HD)]
        copies.append(pltpu.make_async_copy(own_ref, to, sems.at[1, i]))
        copies[-1].start()
    for copy in copies:
        copy.wait()


def lat_kernel(steps_ref, lat_ref, table_ref, pay_ref, coefs_ref):
    table = table_ref[...]
    picked = jnp.where(lane_ids(table.shape) == steps_ref[0], table, 0.0)
    coefs = jnp.broadcast_to(jnp.sum(picked, -1, keepdims=True), (2, LANES))
    c0 = jnp.broadcast_to(coefs[0:1], (8, LANES))
    pay_ref[0] = jnp.concatenate([lat_ref[...], c0], 0)
    coefs_ref[...] = jnp.broadcast_to(coefs[1:2], (8, LANES))


def fill_keys(all_ref, keys, keys_v):
    groups = all_ref.shape[0]
    for j in range(groups):
        block = all_ref[j, :HD]
        width = block.shape[1]
        at = slice(j * width, (j + 1) * width)
        one = jnp.where(row_ids((HD, width)) == 0, 1.0, 0.0)
        keys[at] = jnp.transpose(jnp.concatenate([block.astype(F32), one], 0)).astype(BF16)
        keys_v[:, at] = jnp.concatenate([one.astype(BF16), block], 0)


def fill_queries(heads, maps_of, ex, own_t, queries):
    tokens = own_t.shape[1]
    one = jnp.where(row_ids((HD, tokens)) == 0, 1.0, 0.0).astype(BF16)
    x_only = jnp.concatenate([own_t, jnp.zeros_like(own_t)], 0)
    full = jnp.concatenate([own_t, one], 0)
    ex_t = jnp.transpose(ex.astype(F32))
    consts = jnp.dot(ex, full, preferred_element_type=F32)
    norm = jnp.zeros((1, tokens), F32)
    groups = ex.shape[0] // 16
    for h in range(heads):
        for j in range(groups):
            p = h * groups + j
            row = j * 16 + h
            part = jnp.dot(maps_of(h, j), x_only, preferred_element_type=F32)
            part = part + ex_t[:HD, row : row + 1]
            const = jnp.broadcast_to(consts[row + 4 : row + 5], (HD, tokens))
            const = jnp.where(row_ids((HD, tokens)) == 0, const, 0.0)
            column = jnp.concatenate([part, const], 0).astype(BF16)
            queries[:, p * tokens : (p + 1) * tokens] = column
            column = column.astype(F32)
            norm = jnp.maximum(norm, jnp.sum(column * column, 0, keepdims=True))
    return jnp.max(norm)


def attend(maps_of, groups, tokens, span, query_norm, keys, keys_v, queries, sums):
    aligned = keys_v[...].astype(F32)
    key_norm = jnp.max(jnp.sum(aligned * aligned, 0, keepdims=True))
    safe = query_norm * key_norm <= SAFE * SAFE
    pairs = span // tokens

    def run(terms):
        def step(i, carry):
            at = pl.ds(pl.multiple_of(i * span, span), span)
            s = jnp.dot(keys[...], queries[:, at], preferred_element_type=F32)
            weighted = jnp.dot(keys_v[...], terms(s), preferred_element_type=F32)
            mean = weighted * (1.0 / weighted[:1])
            mean = jnp.where(row_ids(mean.shape) >= HD, mean, 0.0).astype(BF16)
            h, j = lax.div(i * pairs, groups), lax.rem(i * pairs, groups)
            maps = [maps_of(h, j + p) for p in range(pairs)]
            means = [mean[:, p * tokens : (p + 1) * tokens] for p in range(pairs)]
            sums[...] += jnp.dot(
                jnp.concatenate(maps, 1),
                jnp.concatenate(means, 0),
                preferred_element_type=F32,
            )
            return carry

        lax.fori_loop(0, queries.shape[1] // span, step, 0)

    @pl.when(safe)
    def _():
        run(lambda s: jnp.exp2(s).astype(BF16))

    @pl.when(jnp.logical_not(safe))
    def _():
        run(lambda s: jnp.exp2(s - jnp.max(s, 0, keepdims=True)).astype(BF16))


def attend_kernel(
    all_ref, own_ref, cur_ref, w_io_ref, coefs_ref, pay_ref, keys, keys_v, queries, sums, *, span
):
    groups, held, _ = all_ref.shape
    heads = held // HD - 1
    fill_keys(all_ref, keys, keys_v)
    ex = all_ref[:, (1 + heads) * HD :, :].reshape(groups * 16, LANES)
    maps_of = lambda h, j: all_ref[j, (1 + h) * HD : (2 + h) * HD]
    norm = fill_queries(heads, maps_of, ex, own_ref[...], queries)
    ex_t = jnp.transpose(ex.astype(F32))[:HD]
    value = jnp.sum(jnp.where(lane_ids(ex_t.shape) % 16 == 8, ex_t, 0.0), -1, keepdims=True)
    embedded = exact_dot(w_io_ref[...], cur_ref[...].astype(BF16).astype(F32))
    sums[...] = embedded + value

    def maps_at(h, j):
        return all_ref[j, pl.ds(pl.multiple_of((1 + h) * HD, HD), HD)]

    attend(maps_at, groups, own_ref.shape[1], span, norm, keys, keys_v, queries, sums)
    predicted = (coefs_ref[:1] * sums[...]).astype(BF16)
    for i in range(pay_ref.shape[0]):
        pay_ref[i] = predicted


def mirrored(i):
    return (i & 1) * 8 + (i & 2) * 2 + ((i & 4) >> 1) + ((i & 8) >> 3)


def prefix_kernel(pos_ref, pred_ref, lat_ref, start_ref, out_ref, err_ref):
    window = pred_ref.shape[0]
    start = start_ref[...]
    refreshed = start
    current = start
    own = start
    errors = jnp.zeros((1, LANES), F32)
    lanes = lane_ids((1, LANES))
    for s in range(window):
        at = jnp.bitwise_xor(mirrored(pos_ref[0]), mirrored(s))
        refreshed += lat_ref[at, HD : HD + 1] * current + pred_ref[s].astype(F32)
        current = lat_ref[at, :HD]
        difference = refreshed - current
        error = jnp.sum(difference * difference, axis=(0, 1), keepdims=True)
        errors += jnp.where(lanes == s, error, 0.0)
        own = jnp.where(pos_ref[0] == s, refreshed, own)
    out_ref[...] = own
    for i in range(err_ref.shape[0]):
        err_ref[i] = errors


def vmem():
    return pl.BlockSpec(memory_space=pltpu.VMEM)


def smem():
    return pl.BlockSpec(memory_space=pltpu.SMEM)


def params_of(limit):
    return pltpu.CompilerParams(vmem_limit_bytes=limit * MIB)


def on_device(start, latents, time_mod, steps_window, ddim_table, w_in, w_qkv, w_attn_out, w_proj):
    own_rows = start.shape[0]
    window = lax.axis_size("tm")
    groups = lax.axis_size("head")
    d = w_in.shape[1]
    units = w_qkv.shape[1]
    local_heads = units // HD
    seq = groups * own_rows
    pos = lax.axis_index("tm").astype(jnp.int32).reshape(1)
    start_t = start.T
    lat_t = latents[0].T
    table_t = ddim_table.T
    behind_t = lax.ppermute(lat_t, "tm", [(i, i + 1) for i in range(window - 1)])

    lat_pay, coefs = pl.pallas_call(
        lat_kernel,
        in_specs=[smem(), vmem(), vmem()],
        out_specs=[vmem(), vmem()],
        out_shape=[
            jax.ShapeDtypeStruct((1, HD + 8, own_rows), F32),
            jax.ShapeDtypeStruct((8, LANES), F32),
        ],
        compiler_params=params_of(8),
        name="latents",
    )(steps_window, lat_t, table_t)

    held = units + 16
    in_hbm = lambda x: pltpu.with_memory_space_constraint(x, pltpu.HBM)
    hbm = pl.BlockSpec(memory_space=pltpu.HBM)
    params, w_io = pl.pallas_call(
        weights_kernel,
        in_specs=[vmem(), hbm, hbm, hbm, hbm],
        out_specs=[vmem(), vmem()],
        out_shape=[
            jax.ShapeDtypeStruct((held, LANES), BF16),
            jax.ShapeDtypeStruct((HD, HD), F32),
        ],
        scratch_shapes=[
            pltpu.VMEM((HD, d), BF16),
            pltpu.VMEM((3, units, d), BF16),
            pltpu.VMEM((units, d), BF16),
            pltpu.VMEM((HD, d), BF16),
            pltpu.VMEM((2 * LANES, d), BF16),
            pltpu.SemaphoreType.DMA((6,)),
        ],
        compiler_params=params_of(32),
        cost_estimate=pl.CostEstimate(
            flops=2 * d * 4 * units * 256, bytes_accessed=8 * units * d, transcendentals=0
        ),
        name="weights",
    )(
        time_mod.transpose(1, 0, 2),
        in_hbm(w_in),
        in_hbm(w_qkv),
        in_hbm(w_attn_out),
        in_hbm(w_proj.T),
    )

    pay, own, cur_t = pl.pallas_call(
        tokens_kernel,
        in_specs=[smem(), vmem(), vmem(), vmem(), vmem()],
        out_specs=[hbm, vmem(), vmem()],
        out_shape=[
            pltpu.HBM((groups, HD + held, LANES), BF16),
            jax.ShapeDtypeStruct((HD, own_rows), BF16),
            jax.ShapeDtypeStruct((HD, own_rows), F32),
        ],
        scratch_shapes=[pltpu.SemaphoreType.DMA((2, groups))],
        compiler_params=params_of(32),
        name="tokens",
    )(pos, behind_t, start_t, w_in, params)

    gathered = lax.all_to_all(pay, "head", 0, 0, tiled=True)
    lat_all = lat_pay
    for by in (8, 4, 2, 1):
        other = lax.ppermute(lat_all, "tm", [(i, i ^ by) for i in range(window)])
        lat_all = jnp.concatenate([lat_all, other], 0)

    span = 8 * own_rows

    pairs = groups * local_heads * own_rows * seq
    pred_pay = pl.pallas_call(
        functools.partial(attend_kernel, span=span),
        in_specs=[vmem()] * 5,
        out_specs=vmem(),
        out_shape=jax.ShapeDtypeStruct((window, HD, own_rows), BF16),
        scratch_shapes=[
            pltpu.VMEM((seq, LANES), BF16),
            pltpu.VMEM((LANES, seq), BF16),
            pltpu.VMEM((LANES, groups * local_heads * own_rows), BF16),
            pltpu.VMEM((HD, own_rows), F32),
        ],
        compiler_params=params_of(48),
        cost_estimate=pl.CostEstimate(
            flops=1024 * pairs, bytes_accessed=4 * MIB, transcendentals=pairs
        ),
        name="attend",
    )(gathered, own, cur_t, w_io, coefs)

    pred_all = lax.all_to_all(pred_pay, "tm", 0, 0, tiled=True)
    refreshed_t, err_pay = pl.pallas_call(
        prefix_kernel,
        in_specs=[smem(), vmem(), vmem(), vmem()],
        out_specs=[vmem(), vmem()],
        out_shape=[
            jax.ShapeDtypeStruct((HD, own_rows), F32),
            jax.ShapeDtypeStruct((groups, 1, LANES), F32),
        ],
        compiler_params=params_of(32),
        name="prefix",
    )(pos, pred_all, lat_all, start_t)
    errors = lax.all_to_all(err_pay, "head", 0, 0, tiled=True)
    worst = jnp.max(jnp.sum(errors, axis=(0, 1)))
    return refreshed_t.T[None], worst / (seq * HD)


def solution(mesh):
    in_specs = (
        P("head", None),
        P("tm", "head", None),
        P("tm", None, None),
        P("tm"),
        P(),
        P(),
        P(None, "head", None),
        P("head", None),
        P(),
    )
    out_specs = (P("tm", "head", None), P())
    return jax.shard_map(
        on_device, mesh=mesh, in_specs=in_specs, out_specs=out_specs, check_vma=False
    )
```

```python
import functools

import jax
import jax.numpy as jnp
from jax import lax
from jax.experimental import pallas as pl
from jax.experimental.pallas import tpu as pltpu
from jax.sharding import PartitionSpec as P

HD = 64
LANES = 128
LOG2E = 1.4426950408889634
SAFE = 100.0
F32 = jnp.float32
BF16 = jnp.bfloat16
NT = (((1,), (1,)), ((), ()))
MIB = 1 << 20


def lane_ids(shape):
    return lax.broadcasted_iota(jnp.int32, shape, len(shape) - 1)


def row_ids(shape):
    return lax.broadcasted_iota(jnp.int32, shape, 0)


def close_dot(a, b):
    a_head, b_head = a.astype(BF16), b.astype(BF16)
    a_rest = (a - a_head.astype(F32)).astype(BF16)
    b_rest = (b - b_head.astype(F32)).astype(BF16)
    dot = functools.partial(jnp.dot, preferred_element_type=F32)
    return dot(a_head, b_head) + (dot(a_head, b_rest) + dot(a_rest, b_head))


def split_rows(values, before, after):
    head = values.astype(BF16)
    rest = (values - head.astype(F32)).astype(BF16)
    width = values.shape[1]
    parts = []
    for part in (head, rest):
        if before:
            parts.append(jnp.zeros((before, width), BF16))
        parts.append(part)
        if after:
            parts.append(jnp.zeros((after, width), BF16))
    return jnp.concatenate(parts, 0)


def weights_kernel(
    mod_ref, w_in_ref, w_qkv_hbm, w_out_hbm, w_proj_hbm,
    score_ref, value_ref, w_io_ref, w_qkv_ref, w_out_ref, w_proj_ref, tokens_in, sems,
):
    local_heads = w_out_ref.shape[0] // HD
    cols = w_in_ref.shape[1]
    moves = [
        (w_proj_hbm, w_proj_ref),
        (w_out_hbm, w_out_ref),
        (w_qkv_hbm.at[0], w_qkv_ref.at[0]),
        (w_qkv_hbm.at[1], w_qkv_ref.at[1]),
        (w_qkv_hbm.at[2], w_qkv_ref.at[2]),
    ]
    copies = [pltpu.make_async_copy(a, b, sems.at[i]) for i, (a, b) in enumerate(moves)]
    for copy in copies:
        copy.start()

    shift, scale, gate = mod_ref[0], mod_ref[1], mod_ref[2]
    w_in = w_in_ref[...]
    wide = w_in.astype(F32)
    inner = (wide - jnp.mean(wide, -1, keepdims=True)) * (1.0 + scale)
    shift_rows = jnp.where(row_ids((8, cols)) == 0, jnp.broadcast_to(shift, (8, cols)), 0.0)
    tokens_in[...] = split_rows(
        jnp.concatenate([inner, shift_rows], 0), 0, LANES - HD - 8
    )

    def folded(w, by):
        both = lax.dot_general(w, by, NT, preferred_element_type=F32)
        return both[:, :LANES] + both[:, LANES:]

    copies[0].wait()
    w_proj = w_proj_ref[...]
    w_io_ref[...] = lax.dot_general(w_proj, w_in, NT, preferred_element_type=F32)
    gated = split_rows(w_proj.astype(F32) * gate, 0, HD)
    copies[1].wait()
    out = folded(w_out_ref[...], gated)
    units = w_qkv_ref.shape[1]
    for copy in copies[2:]:
        copy.wait()
    proj = folded(w_qkv_ref[...].reshape(3 * units, cols), tokens_in[...])
    proj_q, proj_k, proj_v = proj[:units], proj[units : 2 * units], proj[2 * units :]
    for h in range(local_heads):
        at = slice(h * HD, (h + 1) * HD)
        score = close_dot(jnp.transpose(proj_k[at]), proj_q[at]) * (LOG2E * HD**-0.5)
        value = close_dot(jnp.transpose(out[at])[:HD], proj_v[at])
        score_ref[h] = score.astype(BF16)
        value_ref[h] = value.astype(BF16)


def tokens_kernel(
    last_ref, steps_hbm, lat_hbm, table_hbm, w_in_hbm, start_hbm,
    pay_ref, cur_ref, lat_ref, w_in_ref, start_ref, own_ref, table_ref, steps_ref, sems,
):
    moves = [
        (lat_hbm, lat_ref.at[0, pl.ds(0, HD)]),
        (start_hbm, start_ref),
        (w_in_hbm, w_in_ref),
        (steps_hbm, steps_ref),
        (table_hbm, table_ref),
    ]
    parts = pay_ref.shape[0]
    copies = [pltpu.make_async_copy(a, b, sems.at[parts + i]) for i, (a, b) in enumerate(moves)]
    for copy in copies:
        copy.start()
    for copy in copies[:3]:
        copy.wait()
    current_t = jnp.where(last_ref[0] == 1, start_ref[...], lat_ref[0, :HD])
    cur_ref[...] = current_t
    rounded = jnp.transpose(current_t).astype(BF16)
    hidden = jnp.dot(rounded, w_in_ref[...], preferred_element_type=F32)
    centred = hidden - jnp.mean(hidden, -1, keepdims=True)
    variance = jnp.mean(centred * centred, -1, keepdims=True)
    scaled = rounded.astype(F32) * lax.rsqrt(variance + 1e-05)
    own_ref[...] = jnp.transpose(scaled).astype(BF16)
    sends = [pltpu.make_async_copy(own_ref, pay_ref.at[i], sems.at[i]) for i in range(parts)]
    for send in sends:
        send.start()
    for copy in copies[3:]:
        copy.wait()
    table = table_ref[...]
    picked = jnp.where(lane_ids(table.shape) == steps_ref[0], table, 0.0)
    coefs = jnp.broadcast_to(jnp.sum(picked, -1, keepdims=True), (2, LANES))
    lat_ref[0, pl.ds(HD, 8)] = jnp.concatenate([coefs] * 4, 0)
    for send in sends:
        send.wait()


def attend_kernel(all_ref, score_ref, value_ref, pay_ref, keys, keys_t, queries, sums, *, span):
    groups, _, tokens = all_ref.shape
    heads = score_ref.shape[0]
    seq = keys.shape[0]
    for j in range(groups):
        at = slice(j * tokens, (j + 1) * tokens)
        block = all_ref[j].astype(F32)
        one = jnp.where(row_ids(block.shape) == 0, 1.0, 0.0)
        block = jnp.concatenate([block, one], 0).astype(BF16)
        keys[at] = jnp.transpose(block)
        keys_t[:, at] = block

    def longest(columns):
        columns = columns.astype(F32)
        return jnp.max(jnp.sum(columns * columns, 0, keepdims=True))

    query_norm = 0.0
    for h in range(heads):
        columns = jnp.dot(score_ref[h], keys_t[...], preferred_element_type=F32).astype(BF16)
        queries[h] = columns
        query_norm = jnp.maximum(query_norm, longest(columns))
    safe = query_norm * longest(keys_t[...]) <= SAFE * SAFE
    sums[...] = jnp.zeros_like(sums)

    def run(terms):
        def step(i, carry):
            h = lax.rem(i, heads)
            at = pl.ds(pl.multiple_of(lax.div(i, heads) * span, span), span)
            s = jnp.dot(keys[...], queries[h, :, at], preferred_element_type=F32)
            weighted = jnp.dot(keys_t[...], terms(s), preferred_element_type=F32)
            mean = (weighted * (1.0 / weighted[HD : HD + 1])).astype(BF16)
            sums[:, at] += jnp.dot(value_ref[h], mean, preferred_element_type=F32)
            return carry

        lax.fori_loop(0, heads * (seq // span), step, 0)

    @pl.when(safe)
    def _():
        run(lambda s: jnp.exp2(s).astype(BF16))

    @pl.when(jnp.logical_not(safe))
    def _():
        run(lambda s: jnp.exp2(s - jnp.max(s, 0, keepdims=True)).astype(BF16))

    for j in range(groups):
        pay_ref[j] = sums[:, j * tokens : (j + 1) * tokens].astype(BF16)


def predict_kernel(shares_ref, cur_ref, w_io_ref, pay_ref):
    total = close_dot(w_io_ref[...], cur_ref[...].astype(BF16).astype(F32))
    for j in range(shares_ref.shape[0]):
        total += shares_ref[j].astype(F32)
    predicted = total.astype(BF16)
    for i in range(pay_ref.shape[0]):
        pay_ref[i] = predicted


def mirrored(i):
    return (i & 1) * 8 + (i & 4) + ((i & 8) >> 2) + ((i & 2) >> 1)


def prefix_kernel(pos_ref, pred_ref, lat_ref, start_ref, out_ref, err_ref):
    window = pred_ref.shape[0]
    start = start_ref[...]
    refreshed = start
    current = start
    own = start
    errors = jnp.zeros((1, LANES), F32)
    lanes = lane_ids((1, LANES))
    for s in range(window):
        at = jnp.bitwise_xor(mirrored(pos_ref[0]), mirrored(s))
        predicted = pred_ref[(s - 1) % window].astype(F32)
        c0, c1 = lat_ref[at, HD : HD + 1], lat_ref[at, HD + 1 : HD + 2]
        refreshed += c0 * current + c1 * predicted
        current = lat_ref[at, :HD]
        difference = refreshed - current
        error = jnp.sum(difference * difference, axis=(0, 1), keepdims=True)
        errors += jnp.where(lanes == s, error, 0.0)
        own = jnp.where(pos_ref[0] == s, refreshed, own)
    out_ref[...] = own
    for i in range(err_ref.shape[0]):
        err_ref[i] = errors


def vmem():
    return pl.BlockSpec(memory_space=pltpu.VMEM)


def smem():
    return pl.BlockSpec(memory_space=pltpu.SMEM)


def params_of(limit):
    return pltpu.CompilerParams(vmem_limit_bytes=limit * MIB)


def on_device(start, latents, time_mod, steps_window, ddim_table, w_in, w_qkv, w_attn_out, w_proj):
    own_rows = start.shape[0]
    window = lax.axis_size("tm")
    groups = lax.axis_size("head")
    d = w_in.shape[1]
    units = w_qkv.shape[1]
    local_heads = units // HD
    seq = groups * own_rows
    pos = lax.axis_index("tm").astype(jnp.int32).reshape(1)
    start_t = start.T
    lat_t = latents[0].T
    table_t = ddim_table.T
    mod = time_mod.transpose(1, 0, 2)

    in_hbm = lambda x: pltpu.with_memory_space_constraint(x, pltpu.HBM)
    hbm = pl.BlockSpec(memory_space=pltpu.HBM)
    last = (pos == window - 1).astype(jnp.int32)
    pay, cur_t, lat_pay, w_in_near, start_near = pl.pallas_call(
        tokens_kernel,
        in_specs=[smem(), pl.BlockSpec(memory_space=pl.ANY), hbm, hbm, hbm, hbm],
        out_specs=[hbm] + [vmem()] * 4,
        out_shape=[
            pltpu.HBM((groups, HD, own_rows), BF16),
            pltpu.VMEM((HD, own_rows), F32),
            pltpu.VMEM((1, HD + 8, own_rows), F32),
            pltpu.VMEM((HD, d), BF16),
            pltpu.VMEM((HD, own_rows), F32),
        ],
        scratch_shapes=[
            pltpu.VMEM((HD, own_rows), BF16),
            pltpu.VMEM((2, ddim_table.shape[0]), F32),
            pltpu.SMEM((1,), jnp.int32),
            pltpu.SemaphoreType.DMA((groups + 5,)),
        ],
        compiler_params=params_of(8),
        name="tokens",
    )(last, steps_window, in_hbm(lat_t), in_hbm(table_t), in_hbm(w_in), in_hbm(start_t))
    mod = lax.ppermute(mod, "tm", [(i, (i - 1) % window) for i in range(window)])
    tokens = lax.all_to_all(pay, "head", 0, 0, tiled=True)

    score, value, w_io = pl.pallas_call(
        weights_kernel,
        in_specs=[vmem(), vmem(), hbm, hbm, hbm],
        out_specs=[vmem()] * 3,
        out_shape=[
            jax.ShapeDtypeStruct((local_heads, LANES, LANES), BF16),
            jax.ShapeDtypeStruct((local_heads, HD, LANES), BF16),
            jax.ShapeDtypeStruct((HD, HD), F32),
        ],
        scratch_shapes=[
            pltpu.VMEM((3, units, d), BF16),
            pltpu.VMEM((units, d), BF16),
            pltpu.VMEM((HD, d), BF16),
            pltpu.VMEM((2 * LANES, d), BF16),
            pltpu.SemaphoreType.DMA((5,)),
        ],
        compiler_params=params_of(32),
        cost_estimate=pl.CostEstimate(
            flops=2 * d * 4 * units * 256, bytes_accessed=8 * units * d, transcendentals=0
        ),
        name="weights",
    )(
        mod,
        w_in_near,
        in_hbm(w_qkv),
        in_hbm(w_attn_out),
        in_hbm(w_proj.T),
    )

    pairs = local_heads * seq * seq
    def spread(entries, by):
        other = lax.ppermute(entries, "tm", [(i, i ^ by) for i in range(window)])
        return jnp.concatenate([entries, other], 0)

    lat_all = spread(lat_pay, 2)
    shares = pl.pallas_call(
        functools.partial(attend_kernel, span=seq),
        in_specs=[vmem()] * 3,
        out_specs=vmem(),
        out_shape=jax.ShapeDtypeStruct((groups, HD, own_rows), BF16),
        scratch_shapes=[
            pltpu.VMEM((seq, LANES), BF16),
            pltpu.VMEM((LANES, seq), BF16),
            pltpu.VMEM((local_heads, LANES, seq), BF16),
            pltpu.VMEM((HD, seq), F32),
        ],
        compiler_params=params_of(48),
        cost_estimate=pl.CostEstimate(
            flops=1024 * pairs, bytes_accessed=4 * MIB, transcendentals=pairs
        ),
        name="attend",
    )(tokens, score, value)

    shares, lat_all = lax.optimization_barrier((shares, lat_all))
    lat_all = spread(spread(spread(lat_all, 8), 4), 1)
    shares = lax.all_to_all(shares, "head", 0, 0, tiled=True)

    pred_pay = pl.pallas_call(
        predict_kernel,
        in_specs=[vmem()] * 3,
        out_specs=vmem(),
        out_shape=jax.ShapeDtypeStruct((window, HD, own_rows), BF16),
        compiler_params=params_of(32),
        name="predict",
    )(shares, cur_t, w_io)

    pred_all = lax.all_to_all(pred_pay, "tm", 0, 0, tiled=True)
    refreshed_t, err_pay = pl.pallas_call(
        prefix_kernel,
        in_specs=[smem(), vmem(), vmem(), vmem()],
        out_specs=[vmem(), vmem()],
        out_shape=[
            jax.ShapeDtypeStruct((HD, own_rows), F32),
            jax.ShapeDtypeStruct((groups, 1, LANES), F32),
        ],
        compiler_params=params_of(32),
        name="prefix",
    )(pos, pred_all, lat_all, start_near)
    errors = lax.all_to_all(err_pay, "head", 0, 0, tiled=True)
    worst = jnp.max(jnp.sum(errors, axis=(0, 1)))
    return refreshed_t.T[None], worst / (seq * HD)


def solution(mesh):
    in_specs = (
        P("head", None),
        P("tm", "head", None),
        P("tm", None, None),
        P("tm"),
        P(),
        P(),
        P(None, "head", None),
        P("head", None),
        P(),
    )
    out_specs = (P("tm", "head", None), P())
    return jax.shard_map(
        on_device, mesh=mesh, in_specs=in_specs, out_specs=out_specs, check_vma=False
    )
```

```python
import functools

import jax
import jax.numpy as jnp
from jax import lax
from jax.experimental import pallas as pl
from jax.experimental.pallas import tpu as pltpu
from jax.sharding import PartitionSpec as P

HD = 64
LANES = 128
LOG2E = 1.4426950408889634
SAFE = 100.0
F32 = jnp.float32
BF16 = jnp.bfloat16
NT = (((1,), (1,)), ((), ()))
MIB = 1 << 20


def lane_ids(shape):
    return lax.broadcasted_iota(jnp.int32, shape, len(shape) - 1)


def row_ids(shape):
    return lax.broadcasted_iota(jnp.int32, shape, 0)


def close_dot(a, b):
    a_head, b_head = a.astype(BF16), b.astype(BF16)
    a_rest = (a - a_head.astype(F32)).astype(BF16)
    b_rest = (b - b_head.astype(F32)).astype(BF16)
    dot = functools.partial(jnp.dot, preferred_element_type=F32)
    return dot(a_head, b_head) + (dot(a_head, b_rest) + dot(a_rest, b_head))


def split_rows(values, before, after):
    head = values.astype(BF16)
    rest = (values - head.astype(F32)).astype(BF16)
    width = values.shape[1]
    parts = []
    for part in (head, rest):
        if before:
            parts.append(jnp.zeros((before, width), BF16))
        parts.append(part)
        if after:
            parts.append(jnp.zeros((after, width), BF16))
    return jnp.concatenate(parts, 0)


def weights_kernel(
    mod_ref, w_in_ref, w_qkv_hbm, w_out_hbm, w_proj_hbm,
    score_ref, value_ref, w_io_ref, w_qkv_ref, w_out_ref, w_proj_ref, tokens_in, sems,
):
    local_heads = w_out_ref.shape[0] // HD
    cols = w_in_ref.shape[1]
    moves = [
        (w_proj_hbm, w_proj_ref),
        (w_out_hbm, w_out_ref),
        (w_qkv_hbm.at[0], w_qkv_ref.at[0]),
        (w_qkv_hbm.at[1], w_qkv_ref.at[1]),
        (w_qkv_hbm.at[2], w_qkv_ref.at[2]),
    ]
    copies = [pltpu.make_async_copy(a, b, sems.at[i]) for i, (a, b) in enumerate(moves)]
    for copy in copies:
        copy.start()

    shift, scale, gate = mod_ref[0], mod_ref[1], mod_ref[2]
    w_in = w_in_ref[...]
    wide = w_in.astype(F32)
    inner = (wide - jnp.mean(wide, -1, keepdims=True)) * (1.0 + scale)
    shift_rows = jnp.where(row_ids((8, cols)) == 0, jnp.broadcast_to(shift, (8, cols)), 0.0)
    tokens_in[...] = split_rows(
        jnp.concatenate([inner, shift_rows], 0), 0, LANES - HD - 8
    )

    def folded(w, by):
        both = lax.dot_general(w, by, NT, preferred_element_type=F32)
        return both[:, :LANES] + both[:, LANES:]

    copies[0].wait()
    w_proj = w_proj_ref[...]
    w_io_ref[...] = lax.dot_general(w_proj, w_in, NT, preferred_element_type=F32)
    gated = split_rows(w_proj.astype(F32) * gate, 0, HD)
    copies[1].wait()
    out = folded(w_out_ref[...], gated)
    units = w_qkv_ref.shape[1]
    for copy in copies[2:]:
        copy.wait()
    proj = folded(w_qkv_ref[...].reshape(3 * units, cols), tokens_in[...])
    proj_q, proj_k, proj_v = proj[:units], proj[units : 2 * units], proj[2 * units :]
    for h in range(local_heads):
        at = slice(h * HD, (h + 1) * HD)
        score = close_dot(jnp.transpose(proj_k[at]), proj_q[at]) * (LOG2E * HD**-0.5)
        value = close_dot(jnp.transpose(out[at])[:HD], proj_v[at])
        score_ref[h] = score.astype(BF16)
        value_ref[h] = value.astype(BF16)


def latents_kernel(steps_ref, lat_ref, table_ref, pay_ref):
    table = table_ref[...]
    picked = jnp.where(lane_ids(table.shape) == steps_ref[0], table, 0.0)
    coefs = jnp.broadcast_to(jnp.sum(picked, -1, keepdims=True), (2, LANES))
    pay_ref[0] = jnp.concatenate([lat_ref[...]] + [coefs] * 4, 0)


def tokens_kernel(
    lat_hbm, w_in_hbm, start_hbm, table_hbm,
    pay_ref, cur_ref, w_in_ref, start_ref, lat_ref, table_ref, own_ref, sems,
):
    moves = [
        (lat_hbm, lat_ref),
        (start_hbm, start_ref),
        (w_in_hbm, w_in_ref),
        (table_hbm, table_ref),
    ]
    parts = pay_ref.shape[0]
    copies = [pltpu.make_async_copy(a, b, sems.at[parts + i]) for i, (a, b) in enumerate(moves)]
    for copy in copies:
        copy.start()
    for copy in copies:
        copy.wait()
    last = lax.axis_index("tm") == lax.axis_size("tm") - 1
    current_t = jnp.where(last, start_ref[...], lat_ref[...])
    cur_ref[...] = current_t
    rounded = jnp.transpose(current_t).astype(BF16)
    hidden = jnp.dot(rounded, w_in_ref[...], preferred_element_type=F32)
    centred = hidden - jnp.mean(hidden, -1, keepdims=True)
    variance = jnp.mean(centred * centred, -1, keepdims=True)
    scaled = rounded.astype(F32) * lax.rsqrt(variance + 1e-05)
    own_ref[...] = jnp.transpose(scaled).astype(BF16)
    sends = [pltpu.make_async_copy(own_ref, pay_ref.at[i], sems.at[i]) for i in range(parts)]
    for send in sends:
        send.start()
    for send in sends:
        send.wait()


def attend_kernel(all_ref, score_ref, value_ref, pay_ref, keys, keys_t, queries, sums, *, span):
    groups, _, tokens = all_ref.shape
    heads = score_ref.shape[0]
    seq = keys.shape[0]
    for j in range(groups):
        at = slice(j * tokens, (j + 1) * tokens)
        block = all_ref[j].astype(F32)
        one = jnp.where(row_ids(block.shape) == 0, 1.0, 0.0)
        block = jnp.concatenate([block, one], 0).astype(BF16)
        keys[at] = jnp.transpose(block)
        keys_t[:, at] = block

    def longest(columns):
        columns = columns.astype(F32)
        return jnp.max(jnp.sum(columns * columns, 0, keepdims=True))

    query_norm = 0.0
    for h in range(heads):
        columns = jnp.dot(score_ref[h], keys_t[...], preferred_element_type=F32).astype(BF16)
        queries[h] = columns
        query_norm = jnp.maximum(query_norm, longest(columns))
    safe = query_norm * longest(keys_t[...]) <= SAFE * SAFE
    sums[...] = jnp.zeros_like(sums)

    def run(terms):
        def step(i, carry):
            h = lax.rem(i, heads)
            at = pl.ds(pl.multiple_of(lax.div(i, heads) * span, span), span)
            s = jnp.dot(keys[...], queries[h, :, at], preferred_element_type=F32)
            weighted = jnp.dot(keys_t[...], terms(s), preferred_element_type=F32)
            mean = (weighted * (1.0 / weighted[HD : HD + 1])).astype(BF16)
            sums[:, at] += jnp.dot(value_ref[h], mean, preferred_element_type=F32)
            return carry

        lax.fori_loop(0, heads * (seq // span), step, 0)

    @pl.when(safe)
    def _():
        run(lambda s: jnp.exp2(s).astype(BF16))

    @pl.when(jnp.logical_not(safe))
    def _():
        run(lambda s: jnp.exp2(s - jnp.max(s, 0, keepdims=True)).astype(BF16))

    for j in range(groups):
        pay_ref[j] = sums[:, j * tokens : (j + 1) * tokens].astype(BF16)


def predict_kernel(shares_ref, cur_ref, w_io_ref, pay_ref):
    total = close_dot(w_io_ref[...], cur_ref[...].astype(BF16).astype(F32))
    for j in range(shares_ref.shape[0]):
        total += shares_ref[j].astype(F32)
    predicted = total.astype(BF16)
    for i in range(pay_ref.shape[0]):
        pay_ref[i] = predicted


def mirrored(i):
    return (i & 1) * 8 + (i & 4) + ((i & 8) >> 2) + ((i & 2) >> 1)


def prefix_kernel(pred_ref, lat_ref, start_ref, out_ref, err_ref):
    pos = lax.axis_index("tm")
    window = pred_ref.shape[0]
    start = start_ref[...]
    refreshed = start
    current = start
    own = start
    errors = jnp.zeros((1, LANES), F32)
    lanes = lane_ids((1, LANES))
    for s in range(window):
        at = jnp.bitwise_xor(mirrored(pos), mirrored(s))
        predicted = pred_ref[(s - 1) % window].astype(F32)
        c0, c1 = lat_ref[at, HD : HD + 1], lat_ref[at, HD + 1 : HD + 2]
        refreshed += c0 * current + c1 * predicted
        current = lat_ref[at, :HD]
        difference = refreshed - current
        error = jnp.sum(difference * difference, axis=(0, 1), keepdims=True)
        errors += jnp.where(lanes == s, error, 0.0)
        own = jnp.where(pos == s, refreshed, own)
    out_ref[...] = own
    for i in range(err_ref.shape[0]):
        err_ref[i] = errors


def vmem():
    return pl.BlockSpec(memory_space=pltpu.VMEM)


def smem():
    return pl.BlockSpec(memory_space=pltpu.SMEM)


def params_of(limit):
    return pltpu.CompilerParams(vmem_limit_bytes=limit * MIB)


def on_device(start, latents, time_mod, steps_window, ddim_table, w_in, w_qkv, w_attn_out, w_proj):
    own_rows = start.shape[0]
    window = lax.axis_size("tm")
    groups = lax.axis_size("head")
    d = w_in.shape[1]
    units = w_qkv.shape[1]
    local_heads = units // HD
    seq = groups * own_rows
    start_t = start.T
    lat_t = latents[0].T
    table_t = ddim_table.T
    mod = time_mod.transpose(1, 0, 2)

    in_hbm = lambda x: pltpu.with_memory_space_constraint(x, pltpu.HBM)
    hbm = pl.BlockSpec(memory_space=pltpu.HBM)
    pay, cur_t, w_in_near, start_near, lat_near, table_near = pl.pallas_call(
        tokens_kernel,
        in_specs=[hbm] * 4,
        out_specs=[hbm] + [vmem()] * 5,
        out_shape=[
            pltpu.HBM((groups, HD, own_rows), BF16),
            pltpu.VMEM((HD, own_rows), F32),
            pltpu.VMEM((HD, d), BF16),
            pltpu.VMEM((HD, own_rows), F32),
            pltpu.VMEM((HD, own_rows), F32),
            pltpu.VMEM((2, ddim_table.shape[0]), F32),
        ],
        scratch_shapes=[
            pltpu.VMEM((HD, own_rows), BF16),
            pltpu.SemaphoreType.DMA((groups + 4,)),
        ],
        compiler_params=params_of(8),
        name="tokens",
    )(in_hbm(lat_t), in_hbm(w_in), in_hbm(start_t), in_hbm(table_t))
    lat_pay = pl.pallas_call(
        latents_kernel,
        in_specs=[smem(), vmem(), vmem()],
        out_specs=vmem(),
        out_shape=pltpu.VMEM((1, HD + 8, own_rows), F32),
        compiler_params=params_of(8),
        name="latents",
    )(steps_window, lat_near, table_near)
    mod = lax.ppermute(mod, "tm", [(i, (i - 1) % window) for i in range(window)])
    tokens = lax.all_to_all(pay, "head", 0, 0, tiled=True)

    score, value, w_io = pl.pallas_call(
        weights_kernel,
        in_specs=[vmem(), vmem(), hbm, hbm, hbm],
        out_specs=[vmem()] * 3,
        out_shape=[
            jax.ShapeDtypeStruct((local_heads, LANES, LANES), BF16),
            jax.ShapeDtypeStruct((local_heads, HD, LANES), BF16),
            jax.ShapeDtypeStruct((HD, HD), F32),
        ],
        scratch_shapes=[
            pltpu.VMEM((3, units, d), BF16),
            pltpu.VMEM((units, d), BF16),
            pltpu.VMEM((HD, d), BF16),
            pltpu.VMEM((2 * LANES, d), BF16),
            pltpu.SemaphoreType.DMA((5,)),
        ],
        compiler_params=params_of(32),
        cost_estimate=pl.CostEstimate(
            flops=2 * d * 4 * units * 256, bytes_accessed=8 * units * d, transcendentals=0
        ),
        name="weights",
    )(
        mod,
        w_in_near,
        in_hbm(w_qkv),
        in_hbm(w_attn_out),
        in_hbm(w_proj.T),
    )

    pairs = local_heads * seq * seq
    def spread(entries, by):
        other = lax.ppermute(entries, "tm", [(i, i ^ by) for i in range(window)])
        return jnp.concatenate([entries, other], 0)

    lat_all = spread(lat_pay, 2)
    shares = pl.pallas_call(
        functools.partial(attend_kernel, span=seq),
        in_specs=[vmem()] * 3,
        out_specs=vmem(),
        out_shape=jax.ShapeDtypeStruct((groups, HD, own_rows), BF16),
        scratch_shapes=[
            pltpu.VMEM((seq, LANES), BF16),
            pltpu.VMEM((LANES, seq), BF16),
            pltpu.VMEM((local_heads, LANES, seq), BF16),
            pltpu.VMEM((HD, seq), F32),
        ],
        compiler_params=params_of(48),
        cost_estimate=pl.CostEstimate(
            flops=1024 * pairs, bytes_accessed=4 * MIB, transcendentals=pairs
        ),
        name="attend",
    )(tokens, score, value)

    shares, lat_all = lax.optimization_barrier((shares, lat_all))
    lat_all = spread(spread(spread(lat_all, 8), 4), 1)
    shares = lax.all_to_all(shares, "head", 0, 0, tiled=True)

    pred_pay = pl.pallas_call(
        predict_kernel,
        in_specs=[vmem()] * 3,
        out_specs=vmem(),
        out_shape=jax.ShapeDtypeStruct((window, HD, own_rows), BF16),
        compiler_params=params_of(32),
        name="predict",
    )(shares, cur_t, w_io)

    pred_all = lax.all_to_all(pred_pay, "tm", 0, 0, tiled=True)
    refreshed_t, err_pay = pl.pallas_call(
        prefix_kernel,
        in_specs=[vmem(), vmem(), vmem()],
        out_specs=[vmem(), vmem()],
        out_shape=[
            jax.ShapeDtypeStruct((HD, own_rows), F32),
            jax.ShapeDtypeStruct((groups, 1, LANES), F32),
        ],
        compiler_params=params_of(32),
        name="prefix",
    )(pred_all, lat_all, start_near)
    errors = lax.all_to_all(err_pay, "head", 0, 0, tiled=True)
    worst = jnp.max(jnp.sum(errors, axis=(0, 1)))
    return refreshed_t.T[None], worst / (seq * HD)


def solution(mesh):
    in_specs = (
        P("head", None),
        P("tm", "head", None),
        P("tm", None, None),
        P("tm"),
        P(),
        P(),
        P(None, "head", None),
        P("head", None),
        P(),
    )
    out_specs = (P("tm", "head", None), P())
    return jax.shard_map(
        on_device, mesh=mesh, in_specs=in_specs, out_specs=out_specs, check_vma=False
    )
```

```python
import functools

import jax
import jax.numpy as jnp
from jax import lax
from jax.experimental import pallas as pl
from jax.experimental.pallas import tpu as pltpu
from jax.sharding import PartitionSpec as P

HD = 64
LANES = 128
LOG2E = 1.4426950408889634
SAFE = 100.0
F32 = jnp.float32
BF16 = jnp.bfloat16
NT = (((1,), (1,)), ((), ()))
MIB = 1 << 20


def lane_ids(shape):
    return lax.broadcasted_iota(jnp.int32, shape, len(shape) - 1)


def row_ids(shape):
    return lax.broadcasted_iota(jnp.int32, shape, 0)


def close_dot(a, b):
    a_head, b_head = a.astype(BF16), b.astype(BF16)
    a_rest = (a - a_head.astype(F32)).astype(BF16)
    b_rest = (b - b_head.astype(F32)).astype(BF16)
    dot = functools.partial(jnp.dot, preferred_element_type=F32)
    return dot(a_head, b_head) + (dot(a_head, b_rest) + dot(a_rest, b_head))


def split_rows(values, before, after):
    head = values.astype(BF16)
    rest = (values - head.astype(F32)).astype(BF16)
    width = values.shape[1]
    parts = []
    for part in (head, rest):
        if before:
            parts.append(jnp.zeros((before, width), BF16))
        parts.append(part)
        if after:
            parts.append(jnp.zeros((after, width), BF16))
    return jnp.concatenate(parts, 0)


def weights_kernel(
    mod_ref, w_in_ref, w_qkv_hbm, w_out_hbm, w_proj_hbm,
    score_ref, value_ref, w_io_ref, w_qkv_ref, w_out_ref, w_proj_ref, tokens_in, sems,
):
    local_heads = w_out_ref.shape[0] // HD
    cols = w_in_ref.shape[1]
    moves = [
        (w_proj_hbm, w_proj_ref),
        (w_out_hbm, w_out_ref),
        (w_qkv_hbm.at[0], w_qkv_ref.at[0]),
        (w_qkv_hbm.at[1], w_qkv_ref.at[1]),
        (w_qkv_hbm.at[2], w_qkv_ref.at[2]),
    ]
    copies = [pltpu.make_async_copy(a, b, sems.at[i]) for i, (a, b) in enumerate(moves)]
    for copy in copies:
        copy.start()

    shift, scale, gate = mod_ref[0], mod_ref[1], mod_ref[2]
    w_in = w_in_ref[...]
    wide = w_in.astype(F32)
    inner = (wide - jnp.mean(wide, -1, keepdims=True)) * (1.0 + scale)
    shift_rows = jnp.where(row_ids((8, cols)) == 0, jnp.broadcast_to(shift, (8, cols)), 0.0)
    tokens_in[...] = split_rows(
        jnp.concatenate([inner, shift_rows], 0), 0, LANES - HD - 8
    )

    def folded(w, by):
        both = lax.dot_general(w, by, NT, preferred_element_type=F32)
        return both[:, :LANES] + both[:, LANES:]

    copies[0].wait()
    w_proj = w_proj_ref[...]
    w_io_ref[...] = lax.dot_general(w_proj, w_in, NT, preferred_element_type=F32)
    gated = split_rows(w_proj.astype(F32) * gate, 0, HD)
    copies[1].wait()
    out = folded(w_out_ref[...], gated)
    units = w_qkv_ref.shape[1]
    for copy in copies[2:]:
        copy.wait()
    proj = folded(w_qkv_ref[...].reshape(3 * units, cols), tokens_in[...])
    proj_q, proj_k, proj_v = proj[:units], proj[units : 2 * units], proj[2 * units :]
    for h in range(local_heads):
        at = slice(h * HD, (h + 1) * HD)
        score = close_dot(jnp.transpose(proj_k[at]), proj_q[at]) * (LOG2E * HD**-0.5)
        value = close_dot(jnp.transpose(out[at])[:HD], proj_v[at])
        score_ref[h] = score.astype(BF16)
        value_ref[h] = value.astype(BF16)


def tokens_kernel(
    last_ref, steps_hbm, lat_hbm, table_hbm, w_in_hbm, start_hbm,
    pay_ref, cur_ref, lat_ref, w_in_ref, start_ref, own_ref, table_ref, steps_ref, sems,
):
    moves = [
        (lat_hbm, lat_ref.at[0, pl.ds(0, HD)]),
        (start_hbm, start_ref),
        (w_in_hbm, w_in_ref),
        (steps_hbm, steps_ref),
        (table_hbm, table_ref),
    ]
    parts = pay_ref.shape[0]
    copies = [pltpu.make_async_copy(a, b, sems.at[parts + i]) for i, (a, b) in enumerate(moves)]
    for copy in copies:
        copy.start()
    for copy in copies[:3]:
        copy.wait()
    current_t = jnp.where(last_ref[0] == 1, start_ref[...], lat_ref[0, :HD])
    cur_ref[...] = current_t
    rounded = jnp.transpose(current_t).astype(BF16)
    hidden = jnp.dot(rounded, w_in_ref[...], preferred_element_type=F32)
    centred = hidden - jnp.mean(hidden, -1, keepdims=True)
    variance = jnp.mean(centred * centred, -1, keepdims=True)
    scaled = rounded.astype(F32) * lax.rsqrt(variance + 1e-05)
    own_ref[...] = jnp.transpose(scaled).astype(BF16)
    sends = [pltpu.make_async_copy(own_ref, pay_ref.at[i], sems.at[i]) for i in range(parts)]
    for send in sends:
        send.start()
    for copy in copies[3:]:
        copy.wait()
    table = table_ref[...]
    picked = jnp.where(lane_ids(table.shape) == steps_ref[0], table, 0.0)
    coefs = jnp.broadcast_to(jnp.sum(picked, -1, keepdims=True), (2, LANES))
    lat_ref[0, pl.ds(HD, 8)] = jnp.concatenate([coefs] * 4, 0)
    for send in sends:
        send.wait()


def attend_kernel(all_ref, score_ref, value_ref, pay_ref, keys, keys_t, queries, sums, *, span):
    groups, _, tokens = all_ref.shape
    heads = score_ref.shape[0]
    seq = keys.shape[0]
    for j in range(groups):
        at = slice(j * tokens, (j + 1) * tokens)
        block = all_ref[j].astype(F32)
        one = jnp.where(row_ids(block.shape) == 0, 1.0, 0.0)
        block = jnp.concatenate([block, one], 0).astype(BF16)
        keys[at] = jnp.transpose(block)
        keys_t[:, at] = block

    def longest(columns):
        columns = columns.astype(F32)
        return jnp.max(jnp.sum(columns * columns, 0, keepdims=True))

    query_norm = 0.0
    for h in range(heads):
        columns = jnp.dot(score_ref[h], keys_t[...], preferred_element_type=F32)
        queries[h] = columns.astype(BF16)
        query_norm = jnp.maximum(query_norm, longest(columns))
    safe = query_norm * longest(keys_t[...]) <= SAFE * SAFE
    sums[...] = jnp.zeros_like(sums)

    def run(terms):
        def step(i, carry):
            h = lax.rem(i, heads)
            at = pl.ds(pl.multiple_of(lax.div(i, heads) * span, span), span)
            s = jnp.dot(keys[...], queries[h, :, at], preferred_element_type=F32)
            weighted = jnp.dot(keys_t[...], terms(s), preferred_element_type=F32)
            mean = (weighted * (1.0 / weighted[HD : HD + 1])).astype(BF16)
            sums[:, at] += jnp.dot(value_ref[h], mean, preferred_element_type=F32)
            return carry

        lax.fori_loop(0, heads * (seq // span), step, 0)

    @pl.when(safe)
    def _():
        run(lambda s: jnp.exp2(s).astype(BF16))

    @pl.when(jnp.logical_not(safe))
    def _():
        run(lambda s: jnp.exp2(s - jnp.max(s, 0, keepdims=True)).astype(BF16))

    for j in range(groups):
        pay_ref[j] = sums[:, j * tokens : (j + 1) * tokens].astype(BF16)


def predict_kernel(shares_ref, cur_ref, w_io_ref, pay_ref):
    total = close_dot(w_io_ref[...], cur_ref[...].astype(BF16).astype(F32))
    for j in range(shares_ref.shape[0]):
        total += shares_ref[j].astype(F32)
    predicted = total.astype(BF16)
    for i in range(pay_ref.shape[0]):
        pay_ref[i] = predicted


def mirrored(i):
    return (i & 1) * 8 + (i & 4) + ((i & 8) >> 2) + ((i & 2) >> 1)


def prefix_kernel(pos_ref, pred_ref, lat_ref, start_ref, out_ref, err_ref):
    window = pred_ref.shape[0]
    start = start_ref[...]
    refreshed = start
    current = start
    own = start
    errors = jnp.zeros((1, LANES), F32)
    lanes = lane_ids((1, LANES))
    for s in range(window):
        at = jnp.bitwise_xor(mirrored(pos_ref[0]), mirrored(s))
        predicted = pred_ref[(s - 1) % window].astype(F32)
        c0, c1 = lat_ref[at, HD : HD + 1], lat_ref[at, HD + 1 : HD + 2]
        refreshed += c0 * current + c1 * predicted
        current = lat_ref[at, :HD]
        difference = refreshed - current
        error = jnp.sum(difference * difference, axis=(0, 1), keepdims=True)
        errors += jnp.where(lanes == s, error, 0.0)
        own = jnp.where(pos_ref[0] == s, refreshed, own)
    out_ref[...] = own
    for i in range(err_ref.shape[0]):
        err_ref[i] = errors


def vmem():
    return pl.BlockSpec(memory_space=pltpu.VMEM)


def smem():
    return pl.BlockSpec(memory_space=pltpu.SMEM)


def params_of(limit):
    return pltpu.CompilerParams(vmem_limit_bytes=limit * MIB)


def on_device(start, latents, time_mod, steps_window, ddim_table, w_in, w_qkv, w_attn_out, w_proj):
    own_rows = start.shape[0]
    window = lax.axis_size("tm")
    groups = lax.axis_size("head")
    d = w_in.shape[1]
    units = w_qkv.shape[1]
    local_heads = units // HD
    seq = groups * own_rows
    pos = lax.axis_index("tm").astype(jnp.int32).reshape(1)
    start_t = start.T
    lat_t = latents[0].T
    table_t = ddim_table.T
    mod = time_mod.transpose(1, 0, 2)

    in_hbm = lambda x: pltpu.with_memory_space_constraint(x, pltpu.HBM)
    hbm = pl.BlockSpec(memory_space=pltpu.HBM)
    last = (pos == window - 1).astype(jnp.int32)
    pay, cur_t, lat_pay, w_in_near, start_near = pl.pallas_call(
        tokens_kernel,
        in_specs=[smem(), pl.BlockSpec(memory_space=pl.ANY), hbm, hbm, hbm, hbm],
        out_specs=[hbm] + [vmem()] * 4,
        out_shape=[
            pltpu.HBM((groups, HD, own_rows), BF16),
            pltpu.VMEM((HD, own_rows), F32),
            pltpu.VMEM((1, HD + 8, own_rows), F32),
            pltpu.VMEM((HD, d), BF16),
            pltpu.VMEM((HD, own_rows), F32),
        ],
        scratch_shapes=[
            pltpu.VMEM((HD, own_rows), BF16),
            pltpu.VMEM((2, ddim_table.shape[0]), F32),
            pltpu.SMEM((1,), jnp.int32),
            pltpu.SemaphoreType.DMA((groups + 5,)),
        ],
        compiler_params=params_of(8),
        name="tokens",
    )(last, steps_window, in_hbm(lat_t), in_hbm(table_t), in_hbm(w_in), in_hbm(start_t))
    mod = lax.ppermute(mod, "tm", [(i, (i - 1) % window) for i in range(window)])
    tokens = lax.all_to_all(pay, "head", 0, 0, tiled=True)

    score, value, w_io = pl.pallas_call(
        weights_kernel,
        in_specs=[vmem(), vmem(), hbm, hbm, hbm],
        out_specs=[vmem()] * 3,
        out_shape=[
            jax.ShapeDtypeStruct((local_heads, LANES, LANES), BF16),
            jax.ShapeDtypeStruct((local_heads, HD, LANES), BF16),
            jax.ShapeDtypeStruct((HD, HD), F32),
        ],
        scratch_shapes=[
            pltpu.VMEM((3, units, d), BF16),
            pltpu.VMEM((units, d), BF16),
            pltpu.VMEM((HD, d), BF16),
            pltpu.VMEM((2 * LANES, d), BF16),
            pltpu.SemaphoreType.DMA((5,)),
        ],
        compiler_params=params_of(32),
        cost_estimate=pl.CostEstimate(
            flops=2 * d * 4 * units * 256, bytes_accessed=8 * units * d, transcendentals=0
        ),
        name="weights",
    )(
        mod,
        w_in_near,
        in_hbm(w_qkv),
        in_hbm(w_attn_out),
        in_hbm(w_proj.T),
    )

    pairs = local_heads * seq * seq
    def spread(entries, by):
        other = lax.ppermute(entries, "tm", [(i, i ^ by) for i in range(window)])
        return jnp.concatenate([entries, other], 0)

    lat_all = spread(lat_pay, 2)
    shares = pl.pallas_call(
        functools.partial(attend_kernel, span=seq),
        in_specs=[vmem()] * 3,
        out_specs=vmem(),
        out_shape=jax.ShapeDtypeStruct((groups, HD, own_rows), BF16),
        scratch_shapes=[
            pltpu.VMEM((seq, LANES), BF16),
            pltpu.VMEM((LANES, seq), BF16),
            pltpu.VMEM((local_heads, LANES, seq), BF16),
            pltpu.VMEM((HD, seq), F32),
        ],
        compiler_params=params_of(48),
        cost_estimate=pl.CostEstimate(
            flops=1024 * pairs, bytes_accessed=4 * MIB, transcendentals=pairs
        ),
        name="attend",
    )(tokens, score, value)

    shares, lat_all = lax.optimization_barrier((shares, lat_all))
    lat_all = spread(spread(spread(lat_all, 8), 4), 1)
    shares = lax.all_to_all(shares, "head", 0, 0, tiled=True)

    pred_pay = pl.pallas_call(
        predict_kernel,
        in_specs=[vmem()] * 3,
        out_specs=vmem(),
        out_shape=jax.ShapeDtypeStruct((window, HD, own_rows), BF16),
        compiler_params=params_of(32),
        name="predict",
    )(shares, cur_t, w_io)

    pred_all = lax.all_to_all(pred_pay, "tm", 0, 0, tiled=True)
    refreshed_t, err_pay = pl.pallas_call(
        prefix_kernel,
        in_specs=[smem(), vmem(), vmem(), vmem()],
        out_specs=[vmem(), vmem()],
        out_shape=[
            jax.ShapeDtypeStruct((HD, own_rows), F32),
            jax.ShapeDtypeStruct((groups, 1, LANES), F32),
        ],
        compiler_params=params_of(32),
        name="prefix",
    )(pos, pred_all, lat_all, start_near)
    errors = lax.all_to_all(err_pay, "head", 0, 0, tiled=True)
    worst = jnp.max(jnp.sum(errors, axis=(0, 1)))
    return refreshed_t.T[None], worst / (seq * HD)


def solution(mesh):
    in_specs = (
        P("head", None),
        P("tm", "head", None),
        P("tm", None, None),
        P("tm"),
        P(),
        P(),
        P(None, "head", None),
        P("head", None),
        P(),
    )
    out_specs = (P("tm", "head", None), P())
    return jax.shard_map(
        on_device, mesh=mesh, in_specs=in_specs, out_specs=out_specs, check_vma=False
    )
```
